32 devices in a mesh: dp: 4 (over y, core), tensor: 8 (over z, x).
Axes of the slice: x: 2, y: 2, z: 4, core: 2. Of those that a mesh axis runs over, the one named last changes fastest.
Arguments:
- tokens: bfloat16 [1024, 8192], P('dp', 'tensor'), may hold values from -6 to 6
- pattern: int32 [256, 8], P('tensor'), may hold values from 0 to 63, as said below
- first_blocks: bfloat16 [256, 8, 128, 128], P('tensor'), may hold values from -0.1875 to 0.1875
- second_blocks: bfloat16 [256, 8, 128, 128], P('tensor'), may hold values from -0.1875 to 0.1875
- out_grad: bfloat16 [1024, 8192], P('dp', 'tensor'), may hold values from -0.75 to 0.75
Outputs:
- layer_out: bfloat16 [1024, 8192], P('dp', 'tensor')
- input_grad: bfloat16 [1024, 8192], P('dp', 'tensor')
- first_grad: bfloat16 [256, 8, 128, 128], P('tensor')
- second_grad: bfloat16 [256, 8, 128, 128], P('tensor')
The draws below stay inside these ranges and needn't reach their ends.
Inputs may be any that keep to these rules, and one draw needn't show every extreme that they name: `pattern`: each hidden block row r lists 8 distinct feature blocks: r mod 64, the blocks that differ from it in bit 0, in bit 3 and in the highest bit, and 4 further ones drawn at random. Every feature block is listed by some row.
All inputs are finite; a program needn't handle non-finite values.
Results may differ from the reference program's by a relative error of at most 0.015.
Values may be sent and summed in bfloat16 or wider, within the bound.
No kernel may reach another device: no remote copies, remote signals or barrier semaphores. Data moves between devices by JAX's collectives and lax.ppermute only.
A program may use at most 192 MiB of HBM per device.

```python
import jax
import jax.numpy as jnp
from jax import lax

D = 8192
BLK = 128
K = 8
TOK_DEV = 256
FB = 64
HB = 256
TOKENS = 1024
N_DP = 4
N_TENSOR = 8


def draw_pattern(key, part):
    row_ids = jnp.arange(HB, dtype=jnp.int32)
    base = row_ids % FB
    fixed_cols = jnp.stack([base, base ^ 1, base ^ 8, base ^ FB // 2], axis=1)
    columns = jnp.arange(FB, dtype=jnp.int32)
    scores = jax.random.randint(key, (HB, FB), 0, 1 << 20, dtype=jnp.int32) * FB + columns[None, :]
    taken = jnp.any(fixed_cols[:, :, None] == columns[None, None, :], axis=1)
    scores = jnp.where(taken, -1, scores)
    _, extra = lax.top_k(scores, K - 4)
    return jnp.concatenate([fixed_cols, extra.astype(jnp.int32)], axis=1).astype(jnp.int32)


def steps_of(key, extent, split, smallest, largest):
    def one(position, shards_of):
        heights = jax.random.uniform(jax.random.fold_in(jax.random.fold_in(key, 6), position), (shards_of,), jnp.float32, smallest / len(split), largest / len(split))
        return jnp.repeat(jnp.exp(heights), extent[position] // shards_of).reshape((-1,) + (1,) * (len(extent) - position - 1))

    level = one(*split[0])
    for cut in split[1:]:
        level = level * one(*cut)
    return level


def scatter_about(stream_key, dims, width, most, pieces=(), kind=jnp.bfloat16):
    gain = steps_of(stream_key, dims, pieces, -0.22, 0.18) if pieces else 1.0
    array = jax.random.normal(stream_key, dims, jnp.float32) * width * gain
    return jnp.minimum(jnp.maximum(array, -most), most).astype(kind)


def setup_inputs(seed: int = 0) -> dict:
    arg_keys = jax.random.split(jax.random.key(seed), 6)
    return {
        "tokens": scatter_about(arg_keys[0], (TOKENS, D), 1.0, 6.0, ((0, 4), (1, 8))),
        "pattern": draw_pattern(jax.random.fold_in(arg_keys[5], 71), 0),
        "first_blocks": scatter_about(arg_keys[2], (HB, K, BLK, BLK), (K * BLK) ** -0.5, 0.1875, ((0, 8),)),
        "second_blocks": scatter_about(arg_keys[3], (HB, K, BLK, BLK), (K * BLK) ** -0.5, 0.1875, ((0, 8),)),
        "out_grad": scatter_about(arg_keys[4], (TOKENS, D), 0.125, 0.75, ((0, 4), (1, 8))),
    }


gelu_scale = 0.7978845608028654
gelu_cube = 0.044715


def gelu_pair(value):
    inner = gelu_scale * (value + gelu_cube * value * value * value)
    tangent = jnp.tanh(inner)
    result = 0.5 * value * (1.0 + tangent)
    slope = 0.5 * (1.0 + tangent) + 0.5 * value * (1.0 - tangent * tangent) * gelu_scale * (1.0 + 3.0 * gelu_cube * value * value)
    return result, slope


def rounded(value):
    return lax.optimization_barrier(value.astype(jnp.bfloat16)).astype(jnp.float32)


def reference(tokens, pattern, first_blocks, second_blocks, out_grad):
    highest = lax.Precision.HIGHEST
    features = tokens.reshape(N_DP, TOK_DEV, FB, BLK)
    grads = out_grad.reshape(N_DP, TOK_DEV, FB, BLK)
    group_rows = HB // N_TENSOR
    pattern_groups = pattern.reshape(N_TENSOR, group_rows, K)
    first_groups = first_blocks.reshape(N_TENSOR, group_rows, K, BLK, BLK)
    second_groups = second_blocks.reshape(N_TENSOR, group_rows, K, BLK, BLK)
    columns = jnp.arange(FB, dtype=jnp.int32)

    def step(carry, item):
        out_total, back_total = carry
        rows_pattern, first_part, second_part = item
        first_wide = first_part.astype(jnp.float32)
        second_wide = second_part.astype(jnp.float32)
        select = (rows_pattern[:, :, None] == columns).astype(jnp.float32)
        picked = features[:, :, rows_pattern, :].astype(jnp.float32)
        pre = jnp.einsum('gtrki,rkio->gtro', picked, first_wide)
        value, slope = gelu_pair(pre)
        active = rounded(value)
        contrib = jnp.einsum('gtro,rkoc->gtrkc', active, second_wide)
        out_part = jnp.einsum('gtrkc,rkf->gtfc', contrib, select, precision=highest)
        out_total = out_total + rounded(out_part)
        grad_picked = grads[:, :, rows_pattern, :].astype(jnp.float32)
        act_grad = jnp.einsum('gtrkc,rkoc->gtro', grad_picked, second_wide)
        pre_grad = rounded(act_grad * slope)
        second_term = jnp.sum(rounded(jnp.einsum('gtro,gtrkc->grkoc', active, grad_picked)), axis=0).astype(jnp.bfloat16)
        first_term = jnp.sum(rounded(jnp.einsum('gtrki,gtro->grkio', picked, pre_grad)), axis=0).astype(jnp.bfloat16)
        back_term = jnp.einsum('gtro,rkio->gtrki', pre_grad, first_wide)
        back_part = jnp.einsum('gtrki,rkf->gtfi', back_term, select, precision=highest)
        back_total = back_total + rounded(back_part)
        return (out_total, back_total), (first_term, second_term)

    start = jnp.zeros((N_DP, TOK_DEV, FB, BLK), jnp.float32)
    (out_total, back_total), (first_all, second_all) = lax.scan(step, (start, start), (pattern_groups, first_groups, second_groups))
    layer_out = out_total.reshape(N_DP * TOK_DEV, FB * BLK).astype(jnp.bfloat16)
    input_grad = back_total.reshape(N_DP * TOK_DEV, FB * BLK).astype(jnp.bfloat16)
    first_grad = first_all.reshape(HB, K, BLK, BLK)
    second_grad = second_all.reshape(HB, K, BLK, BLK)
    return (layer_out, input_grad, first_grad, second_grad)
```

```python
import functools

import jax
import jax.numpy as jnp
from jax import lax
from jax.experimental import pallas as pl
from jax.experimental.pallas import tpu as pltpu
from jax.sharding import PartitionSpec as P

gelu_scale = 0.7978845608028654
gelu_cube = 0.044715
BF = jnp.bfloat16
F32 = jnp.float32
ANY = pl.BlockSpec(memory_space=pl.ANY)
VMEM_BYTES = 56 * 1024 * 1024


def gelu_pair(value):
    inner = gelu_scale * (value + gelu_cube * value * value * value)
    tangent = jnp.tanh(inner)
    result = 0.5 * value * (1.0 + tangent)
    slope = 0.5 * (1.0 + tangent) + 0.5 * value * (1.0 - tangent * tangent) * gelu_scale * (
        1.0 + 3.0 * gelu_cube * value * value
    )
    return (result, slope)


def line_pairs(line, step, first, last):
    return [
        (a * 2 + s, (a + step) * 2 + s)
        for a in range(first, last + 1)
        for s in range(2)
        if 0 <= a + step < line
    ]


def swap_pairs(first, last):
    return [(a * 2 + s, a * 2 + 1 - s) for a in range(first, last + 1) for s in range(2)]


def gather_parts(own, line):
    held = {0: own}
    for k in range(1, line):
        held[-k] = lax.ppermute(held[1 - k], "tensor", line_pairs(line, 1, k - 1, line - 2))
        held[k] = lax.ppermute(held[k - 1], "tensor", line_pairs(line, -1, 1, line - k))
    parts = []
    for d in range(1 - line, line):
        across = lax.ppermute(held[d], "tensor", swap_pairs(max(0, -d), min(line - 1, line - 1 - d)))
        parts += [held[d], across]
    return parts


def scatter_sum(send, keep, line):
    got = [lax.ppermute(send[k], "tensor", swap_pairs(0, line - 1)) for k in range(line)]
    both = [keep[k].astype(F32) + got[k].astype(F32) for k in range(line)]
    up = down = None
    for k in range(line - 1, 0, -1):
        load_up, load_down = both[k], both[line - k]
        if up is not None:
            load_up, load_down = load_up + up.astype(F32), load_down + down.astype(F32)
        up = lax.ppermute(load_up.astype(BF), "tensor", line_pairs(line, 1, 0, line - 1 - k))
        down = lax.ppermute(load_down.astype(BF), "tensor", line_pairs(line, -1, k, line - 1))
    total = both[0]
    if up is not None:
        total = total + up.astype(F32) + down.astype(F32)
    return total.astype(BF)


def core_swap(value):
    count = lax.axis_size("dp")
    return lax.ppermute(value, "dp", [(i, i ^ 1) for i in range(count)])


def ring_sum(value):
    count = lax.axis_size("dp")
    total = value.astype(F32)
    for s in range(2, count, 2):
        total = total + lax.ppermute(value, "dp", [(i, (i + s) % count) for i in range(count)]).astype(F32)
    return total.astype(BF)


def load_parts(meta, refs, full, sem, line):
    at, side = meta[0], meta[1]
    for n, ref in enumerate(refs):
        place = at + n // 2 - (line - 1)

        @pl.when((place >= 0) & (place < line))
        def _(ref=ref, place=place, other=n % 2):
            slot = place * 2 + (side if other == 0 else 1 - side)
            pltpu.make_async_copy(ref, full.at[slot], sem).start()


def wait_parts(full, sem):
    pltpu.make_async_copy(full, full, sem).wait()


def block_at(pat, row, j, blocks, own_blocks, size):
    block = pat[row * blocks + j]
    return block // own_blocks, pl.ds(pl.multiple_of((block % own_blocks) * size, size), size)


def pick(full, pat, row, blocks, size):
    own_blocks = full.shape[-1] // size
    pieces = []
    for j in range(blocks):
        shard, lanes = block_at(pat, row, j, blocks, own_blocks, size)
        pieces.append(full[shard, :, lanes])
    return jnp.concatenate(pieces, axis=1)


def forward_kernel(line, n_parts, meta, pat, *refs):
    parts, (w_ref, act_ref, slope_ref, full, sem) = refs[:n_parts], refs[n_parts:]
    row = pl.program_id(0)

    @pl.when(row == 0)
    def _():
        load_parts(meta, parts, full, sem, line)
        wait_parts(full, sem)

    _, blocks, size, _ = w_ref.shape
    picked = pick(full, pat, row, blocks, size)
    pre = jnp.dot(picked, w_ref[0].reshape(blocks * size, size), preferred_element_type=F32)
    value, slope = gelu_pair(pre)
    act_ref[0] = value.astype(BF)
    slope_ref[0] = slope


def forward(meta, pat, parts, weights, line):
    rows, blocks, size, _ = weights.shape
    tok, width = parts[0].shape
    shards = 2 * line
    spec = pl.BlockSpec((1, tok, size), lambda r, *_: (r, 0, 0))
    return pl.pallas_call(
        functools.partial(forward_kernel, line, len(parts)),
        grid_spec=pltpu.PrefetchScalarGridSpec(
            num_scalar_prefetch=2,
            grid=(rows,),
            in_specs=[ANY] * len(parts)
            + [pl.BlockSpec((1, blocks, size, size), lambda r, *_: (r, 0, 0, 0))],
            out_specs=[spec, spec],
            scratch_shapes=[pltpu.VMEM((shards, tok, width), BF), pltpu.SemaphoreType.DMA],
        ),
        out_shape=[
            jax.ShapeDtypeStruct((rows, tok, size), BF),
            jax.ShapeDtypeStruct((rows, tok, size), F32),
        ],
        compiler_params=pltpu.CompilerParams(vmem_limit_bytes=VMEM_BYTES),
        cost_estimate=pl.CostEstimate(
            flops=2 * rows * blocks * tok * size * size,
            bytes_accessed=2 * weights.size + 2 * shards * tok * width + 6 * rows * tok * size,
            transcendentals=rows * tok * size,
        ),
        name="forward_rows",
    )(meta, pat, *parts, weights)


def spread_kernel(flip, line, meta, pat, in_ref, w_ref, send_ref, keep_ref, acc):
    row = pl.program_id(0)
    _, blocks, size, _ = w_ref.shape
    own_blocks = acc.shape[-1] // size

    @pl.when(row == 0)
    def _():
        acc[...] = jnp.zeros_like(acc)

    value = in_ref[0]
    if flip:
        weight = w_ref[0].reshape(blocks * size, size)
        terms = lax.dot_general(value, weight, (((1,), (1,)), ((), ())), preferred_element_type=F32)
    else:
        weight = jnp.concatenate([w_ref[0, j] for j in range(blocks)], axis=1)
        terms = jnp.dot(value, weight, preferred_element_type=F32)
    for j in range(blocks):
        shard, lanes = block_at(pat, row, j, blocks, own_blocks, size)
        acc[shard, :, lanes] += terms[:, j * size : (j + 1) * size]

    @pl.when(row == pl.num_programs(0) - 1)
    def _():
        at, side = meta[0], meta[1]
        for k in range(line):
            place = lax.rem(at + k, line)
            send_ref[k] = acc[place * 2 + 1 - side].astype(BF)
            keep_ref[k] = acc[place * 2 + side].astype(BF)


def spread(flip, meta, pat, values, weights, line, width):
    rows, blocks, size, _ = weights.shape
    tok = values.shape[1]
    whole = pl.BlockSpec((line, tok, width), lambda r, *_: (0, 0, 0))
    return pl.pallas_call(
        functools.partial(spread_kernel, flip, line),
        grid_spec=pltpu.PrefetchScalarGridSpec(
            num_scalar_prefetch=2,
            grid=(rows,),
            in_specs=[
                pl.BlockSpec((1, tok, size), lambda r, *_: (r, 0, 0)),
                pl.BlockSpec((1, blocks, size, size), lambda r, *_: (r, 0, 0, 0)),
            ],
            out_specs=[whole, whole],
            scratch_shapes=[pltpu.VMEM((2 * line, tok, width), F32)],
        ),
        out_shape=[jax.ShapeDtypeStruct((line, tok, width), BF)] * 2,
        compiler_params=pltpu.CompilerParams(vmem_limit_bytes=VMEM_BYTES),
        cost_estimate=pl.CostEstimate(
            flops=2 * rows * blocks * tok * size * size,
            bytes_accessed=2 * weights.size + 2 * values.size + 4 * line * tok * width,
            transcendentals=0,
        ),
        name="spread_back" if flip else "spread_out",
    )(meta, pat, values, weights)


def chunk_row(start, half, meta, i, rows):
    core = meta[2] if half == 0 else 1 - meta[2]
    return core * (rows // 2) + start + i


def chunk_kernel(line, n_parts, start, half, rows, add, chained, meta, pat, *refs):
    g_parts, x_parts, refs = refs[:n_parts], refs[n_parts : 2 * n_parts], refs[2 * n_parts :]
    act_ref, slope_ref, w_ref = refs[:3]
    refs = refs[3:]
    if add:
        more_second, more_first = refs[:2]
        refs = refs[2:]
    if chained:
        refs = refs[1:]
    second_ref, first_ref, pg_ref, g_full, x_full, g_sem, x_sem = refs
    step = pl.program_id(0)
    row = chunk_row(start, half, meta, step, rows)
    _, blocks, size, _ = w_ref.shape

    @pl.when(step == 0)
    def _():
        load_parts(meta, g_parts, g_full, g_sem, line)
        load_parts(meta, x_parts, x_full, x_sem, line)
        wait_parts(g_full, g_sem)

    act = act_ref[0]
    grads = pick(g_full, pat, row, blocks, size)
    second = lax.dot_general(act, grads, (((0,), (0,)), ((), ())), preferred_element_type=F32)
    for j in range(blocks):
        term = second[:, j * size : (j + 1) * size]
        if add:
            term = term.astype(BF).astype(F32) + more_second[0, j].astype(F32)
        second_ref[0, j] = term.astype(BF)
    weight = jnp.concatenate([w_ref[0, j] for j in range(blocks)], axis=1)
    act_grad = lax.dot_general(grads, weight, (((1,), (1,)), ((), ())), preferred_element_type=F32)
    pre_grad = (act_grad * slope_ref[0]).astype(BF)
    pg_ref[0] = pre_grad

    @pl.when(step == 0)
    def _():
        wait_parts(x_full, x_sem)

    picked = pick(x_full, pat, row, blocks, size)
    first = lax.dot_general(picked, pre_grad, (((0,), (0,)), ((), ())), preferred_element_type=F32)
    for j in range(blocks):
        term = first[j * size : (j + 1) * size]
        if add:
            term = term.astype(BF).astype(F32) + more_first[0, j].astype(F32)
        first_ref[0, j] = term.astype(BF)


def chunk(meta, pat, g_parts, x_parts, act, slope, weights, more, pg, start, count, half, line):
    rows, blocks, size, _ = weights.shape
    tok, width = g_parts[0].shape
    n = len(g_parts)

    def at_row(r, meta, pat):
        return (chunk_row(start, half, meta, r, rows), 0, 0)

    row_spec = pl.BlockSpec((1, tok, size), at_row)
    block_spec = pl.BlockSpec((1, blocks, size, size), lambda r, *_: (r, 0, 0, 0))
    w_spec = pl.BlockSpec((1, blocks, size, size), lambda r, m, p: at_row(r, m, p) + (0,))
    args = [*g_parts, *x_parts, act, slope, weights]
    specs = [ANY] * (2 * n) + [row_spec, row_spec, w_spec]
    if more is not None:
        args += list(more)
        specs += [block_spec, block_spec]
    aliases = {}
    if pg is not None:
        aliases = {2 + len(args): 2}
        args.append(pg)
        specs.append(ANY)
    grad = jax.ShapeDtypeStruct((count, blocks, size, size), BF)
    return pl.pallas_call(
        functools.partial(chunk_kernel, line, n, start, half, rows, more is not None, pg is not None),
        grid_spec=pltpu.PrefetchScalarGridSpec(
            num_scalar_prefetch=2,
            grid=(count,),
            in_specs=specs,
            out_specs=[block_spec, block_spec, row_spec],
            scratch_shapes=[
                pltpu.VMEM((2 * line, tok, width), BF),
                pltpu.VMEM((2 * line, tok, width), BF),
                pltpu.SemaphoreType.DMA,
                pltpu.SemaphoreType.DMA,
            ],
        ),
        out_shape=[grad, grad, jax.ShapeDtypeStruct((rows, tok, size), BF)],
        input_output_aliases=aliases,
        compiler_params=pltpu.CompilerParams(vmem_limit_bytes=VMEM_BYTES),
        cost_estimate=pl.CostEstimate(
            flops=6 * count * blocks * tok * size * size,
            bytes_accessed=8 * line * tok * width + 6 * count * blocks * size * size,
            transcendentals=0,
        ),
        name="grad_rows",
    )(meta, pat, *args)


def shards(tokens, pattern, first_blocks, second_blocks, out_grad):
    rows, blocks, size, _ = first_blocks.shape
    width = tokens.shape[1]
    line = lax.axis_size("tensor") // 2
    place = lax.axis_index("tensor")
    core = lax.axis_index("dp") % 2
    meta = jnp.stack([place // 2, place % 2, core]).astype(jnp.int32)
    pat = pattern.reshape(-1)

    x_parts = gather_parts(tokens, line)
    g_parts = gather_parts(out_grad, line)
    act, slope = forward(meta, pat, x_parts, first_blocks, line)
    out_send, out_keep = spread(False, meta, pat, act, second_blocks, line, width)

    half_rows = rows // 2
    count = max(1, half_rows // 4)
    starts = list(range(0, half_rows, count))
    run = functools.partial(chunk, meta, pat, g_parts, x_parts, act, slope, second_blocks)
    pg = None
    sent, kept = {}, {}
    for n in range(len(starts) + 1):
        if n < len(starts):
            second, first, pg = run(None, pg, starts[n], count, 1, line)
            sent[n] = (core_swap(second), core_swap(first))
        if n > 0:
            second, first, pg = run(sent[n - 1], pg, starts[n - 1], count, 0, line)
            kept[n - 1] = (second, first)
    back_send, back_keep = spread(True, meta, pat, pg, first_blocks, line, width)

    layer_out = scatter_sum(out_send, out_keep, line)
    input_grad = scatter_sum(back_send, back_keep, line)

    totals = [jnp.zeros(first_blocks.shape, BF), jnp.zeros(first_blocks.shape, BF)]
    for n, start in enumerate(starts):
        for which in range(2):
            own = ring_sum(kept[n][which])
            other = core_swap(own)
            total = totals[which]
            total = lax.dynamic_update_slice(total, own, (core * half_rows + start, 0, 0, 0))
            total = lax.dynamic_update_slice(total, other, ((1 - core) * half_rows + start, 0, 0, 0))
            totals[which] = total
    return (layer_out, input_grad, totals[1], totals[0])


def solution(mesh):
    placed = (
        P("dp", "tensor"),
        P("tensor", None),
        P("tensor", None, None, None),
        P("tensor", None, None, None),
        P("dp", "tensor"),
    )
    return jax.shard_map(
        shards,
        mesh=mesh,
        in_specs=placed,
        out_specs=(
            P("dp", "tensor"),
            P("dp", "tensor"),
            P("tensor", None, None, None),
            P("tensor", None, None, None),
        ),
        check_vma=False,
    )
```

```python
import functools
import math

import jax
import jax.numpy as jnp
from jax import lax
from jax.experimental import pallas as pl
from jax.experimental.pallas import tpu as pltpu
from jax.sharding import PartitionSpec as P

gelu_scale = 0.7978845608028654
gelu_cube = 0.044715
BF = jnp.bfloat16
F32 = jnp.float32
ANY = pl.BlockSpec(memory_space=pl.ANY)
VMEM_BYTES = 56 * 1024 * 1024
small_cost = pl.CostEstimate(flops=1000, bytes_accessed=1000, transcendentals=0)


def gelu_pair(value):
    inner = gelu_scale * (value + gelu_cube * value * value * value)
    tangent = jnp.tanh(inner)
    result = 0.5 * value * (1.0 + tangent)
    slope = 0.5 * (1.0 + tangent) + 0.5 * value * (1.0 - tangent * tangent) * gelu_scale * (
        1.0 + 3.0 * gelu_cube * value * value
    )
    return (result, slope)


def line_pairs(line, step, first, last):
    return [
        (a * 2 + s, (a + step) * 2 + s)
        for a in range(first, last + 1)
        for s in range(2)
        if 0 <= a + step < line
    ]


def swap_pairs(first, last):
    return [(a * 2 + s, a * 2 + 1 - s) for a in range(first, last + 1) for s in range(2)]


def tie(value, others):
    return lax.optimization_barrier((value, others)) if others else (value, others)


def gather_parts(own, line):
    middle = line // 2
    held = {0: (own, own)}
    parts = [(own, 0, 0, 0, line - 1)]
    crossed, places, later = [], [], []
    for step in range(1, line + 1):
        k = step - 1
        (from_up, from_down), crossed = tie(held[k], crossed)
        for n, got in zip(places, crossed):
            parts[n] = (got,) + parts[n][1:]
        places = []
        if step < line:
            up = lax.ppermute(from_up, "tensor", line_pairs(line, 1, k, line - 2))
            down = lax.ppermute(from_down, "tensor", line_pairs(line, -1, 1, line - 1 - k))
            held[step] = (up, down)
            parts += [(up, -step, 0, step, line - 1), (down, step, 0, 0, line - 1 - step)]
        if k == 0:
            moves, after = [(own, 0, 0, line - 1)], []
        else:
            moves = [
                (from_down, k, 0, min(middle - 1, line - 1 - k)),
                (from_up, -k, max(middle, k), line - 1),
            ]
            after = [(from_up, -k, k, middle - 1), (from_down, k, middle, line - 1 - k)]
        crossed = []
        for value, d, first, last in moves + later:
            if first <= last:
                got = lax.ppermute(value, "tensor", swap_pairs(first, last))
                places.append(len(parts))
                parts.append((got, d, 1, first, last))
                crossed.append(got)
        later = after
    for value, d, first, last in later:
        if first <= last:
            got = lax.ppermute(value, "tensor", swap_pairs(first, last))
            parts.append((got, d, 1, first, last))
    return parts


class Order:
    def __init__(self, last):
        self.last = [last]

    def kernel(self, call, *args, also=()):
        out = call([*self.last, *also], *args)
        self.last = [jax.tree.leaves(out)[0]]
        return out


    def fusion(self, call, *args):
        args, before = tie(args, self.last)
        out = call(*args)
        self.last = [jax.tree.leaves(out)[0], *before]
        return out


def far_first(line):
    return sorted(range(line), key=lambda k: (-max(k, line - k) if k else 0, -k))


class LineSum:
    def __init__(self, keep, send):
        self.line, self.keep, self.k = keep.shape[0], keep, keep.shape[0] - 1
        self.got = [lax.ppermute(part, "tensor", swap_pairs(0, self.line - 1)) for part in send]
        self.moved = []

    def across(self, k):
        n = far_first(self.line).index(k)
        return self.got[2 * n // self.line], n % (self.line // 2)

    def step(self, order):
        k, line = self.k, self.line

        def both(k, keep, got):
            return keep[k].astype(F32) + got[self.across(k)[1]].astype(F32)

        if k > 0:

            def loads(keep, got_up, got_down, *moved):
                out = [both(k, keep, got_up), both(line - k, keep, got_down)]
                if moved:
                    out = [a + b.astype(F32) for a, b in zip(out, moved)]
                return [a.astype(BF) for a in out]

            got = self.across(k)[0], self.across(line - k)[0]
            up, down = order.fusion(loads, self.keep, *got, *self.moved)
            self.moved = [
                lax.ppermute(up, "tensor", line_pairs(line, 1, 0, line - 1 - k)),
                lax.ppermute(down, "tensor", line_pairs(line, -1, k, line - 1)),
            ]
        else:

            def last(keep, got, *moved):
                total = both(0, keep, got)
                for a in moved:
                    total = total + a.astype(F32)
                return total.astype(BF)

            self.total = order.fusion(last, self.keep, self.across(0)[0], *self.moved)
        self.k -= 1

    def finished(self):
        return self.k < 0


def core_swap(value):
    count = lax.axis_size("dp")
    return lax.ppermute(value, "dp", [(i, i ^ 1) for i in range(count)])


def ring_parts(value):
    count = lax.axis_size("dp")
    parts = [value]
    for t in range(2, count, 2):
        parts.append(lax.ppermute(value, "dp", [(i, (i + t) % count) for i in range(count)]))
    if len(parts) > 2:
        ring = lax.axis_index("dp") // 2
        stacked = jnp.stack(parts)
        parts = [
            lax.dynamic_index_in_dim(stacked, (ring - y) % len(parts), keepdims=False)
            for y in range(len(parts))
        ]
    return parts


def load_parts(meta, which, ranges, refs, full, sem):
    at, side = meta[0], meta[1]
    for (offset, other, first, last), ref in zip(ranges, refs):

        @pl.when((at >= first) & (at <= last))
        def _(offset=offset, other=other, ref=ref):
            slot = (at + offset) * 2 + (1 - side if other else side)
            pltpu.make_async_copy(ref.at[which], full.at[slot], sem).start()


def wait_parts(full, sem):
    pltpu.make_async_copy(full, full, sem).wait()


def block_at(pat, row, j, blocks, own_blocks, size):
    block = pat[row * blocks + j]
    return block // own_blocks, pl.ds(pl.multiple_of((block % own_blocks) * size, size), size)


def pick(full, pat, row, blocks, size):
    own_blocks = full.shape[-1] // size
    pieces = []
    for j in range(blocks):
        shard, lanes = block_at(pat, row, j, blocks, own_blocks, size)
        pieces.append(full[shard, :, lanes])
    return jnp.concatenate(pieces, axis=1)


def forward_kernel(ranges, meta, pat, *refs):
    parts, refs = refs[: len(ranges)], refs[len(ranges) :]
    w_ref, act_ref, slope_ref, full, sem = refs
    row = pl.program_id(0)

    @pl.when(row == 0)
    def _():
        load_parts(meta, 0, ranges, parts, full, sem)
        wait_parts(full, sem)

    together, blocks, size, _ = w_ref.shape
    for i in range(together):
        picked = pick(full, pat, row * together + i, blocks, size)
        pre = jnp.dot(picked, w_ref[i].reshape(blocks * size, size), preferred_element_type=F32)
        value, slope = gelu_pair(pre)
        act_ref[i] = value.astype(BF)
        slope_ref[i] = slope


def forward(meta, pat, parts, weights, line):
    rows, blocks, size, _ = weights.shape
    parts, ranges = [p[0] for p in parts], [p[1:] for p in parts]
    _, tok, width = parts[0].shape
    shards = 2 * line
    together = math.gcd(rows, 8)
    spec = pl.BlockSpec((together, tok, size), lambda r, *_: (r, 0, 0))
    return pl.pallas_call(
        functools.partial(forward_kernel, ranges),
        grid_spec=pltpu.PrefetchScalarGridSpec(
            num_scalar_prefetch=2,
            grid=(rows // together,),
            in_specs=[ANY] * len(parts)
            + [pl.BlockSpec((together, blocks, size, size), lambda r, *_: (r, 0, 0, 0))],
            out_specs=[spec, spec],
            scratch_shapes=[pltpu.VMEM((shards, tok, width), BF), pltpu.SemaphoreType.DMA],
        ),
        out_shape=[
            jax.ShapeDtypeStruct((rows, tok, size), BF),
            jax.ShapeDtypeStruct((rows, tok, size), F32),
        ],
        compiler_params=pltpu.CompilerParams(vmem_limit_bytes=VMEM_BYTES),
        cost_estimate=small_cost,
        name="forward_rows",
    )(meta, pat, *parts, weights)


def spread_kernel(flip, n_after, line, meta, pat, *refs):
    in_ref, w_ref, *out_refs, acc = refs[n_after:]
    step = pl.program_id(0)
    together, blocks, size, _ = w_ref.shape
    own_blocks = acc.shape[-1] // size

    @pl.when(step == 0)
    def _():
        acc[...] = jnp.zeros_like(acc)

    for i in range(together):
        value = in_ref[i]
        if flip:
            weight = w_ref[i].reshape(blocks * size, size)
            terms = lax.dot_general(
                value, weight, (((1,), (1,)), ((), ())), preferred_element_type=F32
            )
        else:
            weight = jnp.concatenate([w_ref[i, j] for j in range(blocks)], axis=1)
            terms = jnp.dot(value, weight, preferred_element_type=F32)
        for j in range(blocks):
            shard, lanes = block_at(pat, step * together + i, j, blocks, own_blocks, size)
            acc[shard, :, lanes] += terms[:, j * size : (j + 1) * size]

    @pl.when(step == pl.num_programs(0) - 1)
    def _():
        keep_ref, *send_refs = out_refs
        at, side = meta[0], meta[1]
        for n, k in enumerate(far_first(line)):
            place = lax.rem(at + k, line) * 2
            keep_ref[k] = acc[place + side].astype(BF)
            send_refs[2 * n // line][n % (line // 2)] = acc[place + 1 - side].astype(BF)


def spread(flip, meta, pat, line, width, after, values, weights):
    rows, blocks, size, _ = weights.shape
    tok = values.shape[1]
    together = math.gcd(rows, 4)
    whole = (2 * line, tok, width)
    shapes = [(line, tok, width)] + [(line // 2, tok, width)] * 2
    return pl.pallas_call(
        functools.partial(spread_kernel, flip, len(after), line),
        grid_spec=pltpu.PrefetchScalarGridSpec(
            num_scalar_prefetch=2,
            grid=(rows // together,),
            in_specs=[
                *[ANY] * len(after),
                pl.BlockSpec((together, tok, size), lambda r, *_: (r, 0, 0)),
                pl.BlockSpec((together, blocks, size, size), lambda r, *_: (r, 0, 0, 0)),
            ],
            out_specs=[pl.BlockSpec(d, lambda r, *_, n=len(d): (0,) * n) for d in shapes],
            scratch_shapes=[pltpu.VMEM(whole, F32)],
        ),
        out_shape=[jax.ShapeDtypeStruct(d, BF) for d in shapes],
        compiler_params=pltpu.CompilerParams(vmem_limit_bytes=VMEM_BYTES),
        cost_estimate=small_cost,
        name="spread_back" if flip else "spread_out",
    )(meta, pat, *after, values, weights)


def chunk_row(start, half, meta, i, rows):
    core = meta[2] if half == 0 else 1 - meta[2]
    return core * (rows // 2) + start + i


def chunk_kernel(n_after, ranges, spans, start, half, rows, chained, meta, pat, *refs):
    refs = refs[n_after:]
    parts, refs = refs[: len(ranges)], refs[len(ranges) :]
    act_ref, slope_ref, w_ref = refs[:3]
    more, refs = (refs[3 : 3 + 2 * len(spans)], refs[3 + 2 * len(spans) :]) if half == 0 else ((), refs[3:])
    refs = refs[1:] if chained else refs
    *outs, pg_ref, g_full, x_full, g_sem, x_sem = refs
    step = pl.program_id(0)
    together, blocks, size, _ = w_ref.shape
    row = chunk_row(start, half, meta, step * together, rows)

    @pl.when(step == 0)
    def _():
        load_parts(meta, 1, ranges, parts, g_full, g_sem)
        load_parts(meta, 0, ranges, parts, x_full, x_sem)
        wait_parts(g_full, g_sem)

    def store(n, which, i, terms):
        for j, term in enumerate(terms):
            if half == 0:
                term = term.astype(F32) + more[2 * n + which][i, j].astype(F32)
                outs[n][which, i, j] = term.astype(BF)
            else:
                outs[2 * n + which][i, j] = term

    def work(n):
        for i in range(together):
            grads = pick(g_full, pat, row + i, blocks, size)
            second = lax.dot_general(
                act_ref[i], grads, (((0,), (0,)), ((), ())), preferred_element_type=F32
            ).astype(BF)
            store(n, 0, i, [second[:, j * size : (j + 1) * size] for j in range(blocks)])
            weight = jnp.concatenate([w_ref[i, j] for j in range(blocks)], axis=1)
            act_grad = lax.dot_general(
                grads, weight, (((1,), (1,)), ((), ())), preferred_element_type=F32
            )
            pg_ref[i] = (act_grad * slope_ref[i]).astype(BF)
        if n == 0:

            @pl.when(step == 0)
            def _():
                wait_parts(x_full, x_sem)

        for i in range(together):
            picked = pick(x_full, pat, row + i, blocks, size)
            first = lax.dot_general(
                picked, pg_ref[i], (((0,), (0,)), ((), ())), preferred_element_type=F32
            ).astype(BF)
            store(n, 1, i, [first[j * size : (j + 1) * size] for j in range(blocks)])

    if len(spans) == 1:
        return work(0)
    for n, (low, count) in enumerate(spans):
        inside = (step >= low // together) & (step < (low + count) // together)
        pl.when(inside)(functools.partial(work, n))


def chunk(meta, pat, parts, act, slope, weights, line, start, counts, half, after, more, pg):
    rows, blocks, size, _ = weights.shape
    parts, ranges = [p[0] for p in parts], [p[1:] for p in parts]
    _, tok, width = parts[0].shape
    spans = [(sum(counts[:n]), count) for n, count in enumerate(counts)]
    together = math.gcd(start, rows // 2, 4, *counts)

    def at_row(r, meta, pat):
        return (chunk_row(start, half, meta, r * together, rows) // together, 0, 0)

    def in_span(low, count, lead):
        def index(r, *_):
            return lead + (jnp.clip(r - low // together, 0, count // together - 1), 0, 0, 0)

        return pl.BlockSpec((2,) * len(lead) + (together, blocks, size, size), index)

    row_spec = pl.BlockSpec((together, tok, size), at_row)
    w_spec = pl.BlockSpec((together, blocks, size, size), lambda r, m, p: at_row(r, m, p) + (0,))
    args = [*after, *parts, act, slope, weights]
    specs = [ANY] * (len(after) + len(parts)) + [row_spec, row_spec, w_spec]
    out_specs, out_shape = [], []
    for low, count in spans:
        if half == 0:
            specs += [in_span(low, count, ())] * 2
            out_specs.append(in_span(low, count, (0,)))
            out_shape.append(jax.ShapeDtypeStruct((2, count, blocks, size, size), BF))
        else:
            out_specs += [in_span(low, count, ())] * 2
            out_shape += [jax.ShapeDtypeStruct((count, blocks, size, size), BF)] * 2
    if half == 0:
        args += more
    aliases = {}
    if pg is not None:
        aliases = {2 + len(args): len(out_shape)}
        args.append(pg)
        specs.append(ANY)
    full = pltpu.VMEM((2 * line, tok, width), BF)
    *outs, pg = pl.pallas_call(
        functools.partial(
            chunk_kernel, len(after), ranges, spans, start, half, rows, pg is not None
        ),
        grid_spec=pltpu.PrefetchScalarGridSpec(
            num_scalar_prefetch=2,
            grid=(sum(counts) // together,),
            in_specs=specs,
            out_specs=out_specs + [row_spec],
            scratch_shapes=[full, full, pltpu.SemaphoreType.DMA, pltpu.SemaphoreType.DMA],
        ),
        out_shape=out_shape + [jax.ShapeDtypeStruct((rows, tok, size), BF)],
        input_output_aliases=aliases,
        compiler_params=pltpu.CompilerParams(vmem_limit_bytes=VMEM_BYTES),
        cost_estimate=small_cost,
        name="grad_rows",
    )(meta, pat, *args)
    return outs, pg


def place_kernel(n_after, total, chained, meta, *refs):
    refs = refs[n_after:]
    in_refs, refs = refs[:total], refs[total + (2 if chained else 0) + 1 :]
    for which in range(2):
        if len(refs) == 2:
            value = in_refs[which][...]
        else:
            value = in_refs[0][which].astype(F32)
            for ref in in_refs[1:]:
                value = value + ref[which].astype(F32)
            value = value.astype(BF)
            refs[2 + which][...] = value
        refs[which][...] = value


def place(meta, shape, start, half, after, parts, into):
    rows, blocks, size, _ = shape
    adding = half == 0
    count = parts[0].shape[1 if adding else 0]
    together = math.gcd(count, start, 2, rows // 2)
    n = len(parts)

    def at_row(r, meta):
        return (chunk_row(start, half, meta, r * together, rows) // together, 0, 0, 0)

    pair_spec = pl.BlockSpec((2, together, blocks, size, size), lambda r, *_: (0, r, 0, 0, 0))
    one_spec = pl.BlockSpec((together, blocks, size, size), lambda r, *_: (r, 0, 0, 0))
    out_spec = pl.BlockSpec((together, blocks, size, size), at_row)
    out_shape = [jax.ShapeDtypeStruct((8, 128), jnp.int32)] + [jax.ShapeDtypeStruct(shape, BF)] * 2
    out_specs = [ANY, out_spec, out_spec]
    if adding:
        out_shape += [jax.ShapeDtypeStruct(parts[0].shape[1:], BF)] * 2
        out_specs += [one_spec, one_spec]
    args = [*after, *parts]
    specs = [ANY] * len(after) + [pair_spec if adding else one_spec] * n
    aliases = {}
    if into is not None:
        aliases = {1 + len(args): 1, 2 + len(args): 2}
        args += into
        specs += [ANY, ANY]
    _, second, first, *own = pl.pallas_call(
        functools.partial(place_kernel, len(after), n, into is not None),
        grid_spec=pltpu.PrefetchScalarGridSpec(
            num_scalar_prefetch=1,
            grid=(count // together,),
            in_specs=specs,
            out_specs=out_specs,
        ),
        out_shape=out_shape,
        input_output_aliases=aliases,
        compiler_params=pltpu.CompilerParams(vmem_limit_bytes=VMEM_BYTES),
        cost_estimate=small_cost,
        name="place_rows",
    )(meta, *args)
    return _, [second, first], own


def chunk_counts(half_rows):
    unit = half_rows // 8
    if unit and half_rows == 8 * unit:
        return [unit, 4 * unit, 2 * unit, unit]
    return [1] * half_rows


def shards(tokens, pattern, first_blocks, second_blocks, out_grad):
    rows, blocks, size, _ = first_blocks.shape
    width = tokens.shape[1]
    line = lax.axis_size("tensor") // 2
    where = lax.axis_index("tensor")
    core = lax.axis_index("dp") % 2
    meta = jnp.stack([where // 2, where % 2, core]).astype(jnp.int32)
    pat = pattern.reshape(-1)

    half_rows = rows // 2
    counts = chunk_counts(half_rows)
    starts = [sum(counts[:n]) for n in range(len(counts))]
    chunks = range(len(counts))

    parts = gather_parts(jnp.stack([tokens, out_grad]), line)
    act, slope = forward(meta, pat, parts, first_blocks, line)
    order = Order(act)

    def grad_rows(first, last, half, more, pg):
        run = functools.partial(
            chunk, meta, pat, parts, act, slope, second_blocks, line, starts[first],
            counts[first:last], half,
        )
        return order.kernel(run, more, pg)

    def sum_half(first, last, pg):
        outs, pg = grad_rows(first, last, 0, [s for pair in sent[first:last] for s in pair], pg)
        if first > 0:
            outs[0], kept[0][1:] = tie(outs[0], kept[0][1:])
        return [ring_parts(grads) for grads in outs], pg

    def other_half(first, last, pg):
        outs, pg = grad_rows(first, last, 1, None, pg)
        swapped = [core_swap(grads) for grads in outs]
        return [swapped[n : n + 2] for n in range(0, len(swapped), 2)], pg

    last = len(counts)
    sent, pg = other_half(0, last, None)
    kept, pg = sum_half(0, 1, pg)
    if last > 1:
        more, pg = sum_half(1, last, pg)
        kept += more

    totals, own = None, {}

    def settle(n, totals, also=()):
        run = functools.partial(place, meta, first_blocks.shape, starts[n], 0)
        _, totals, one = order.kernel(run, kept[n], totals, also=also)
        own[n] = [core_swap(v) for v in one]
        return totals

    def settle_other(n, totals):
        run = functools.partial(place, meta, first_blocks.shape, starts[n], 1)
        return order.kernel(run, own[n], totals)[1]

    totals = settle(0, totals)
    sums = []
    for flip, values, weights in ((False, act, second_blocks), (True, pg, first_blocks)):
        run = functools.partial(spread, flip, meta, pat, line, width)
        keep, *send = order.kernel(run, values, weights)
        sums.append(LineSum(keep, send))
    out, back = sums
    while out.k > 0:
        out.step(order)
    back.step(order)
    for n in range(1, last):
        totals = settle(n, totals)
        totals = settle_other(n - 1, totals)
        for item in (out, back, back):
            if not item.finished():
                item.step(order)
    for item in (out, back):
        while not item.finished():
            item.step(order)
    totals = settle_other(last - 1, totals)
    return (out.total, back.total, totals[1], totals[0])


def solution(mesh):
    placed = (
        P("dp", "tensor"),
        P("tensor", None),
        P("tensor", None, None, None),
        P("tensor", None, None, None),
        P("dp", "tensor"),
    )
    return jax.shard_map(
        shards,
        mesh=mesh,
        in_specs=placed,
        out_specs=(
            P("dp", "tensor"),
            P("dp", "tensor"),
            P("tensor", None, None, None),
            P("tensor", None, None, None),
        ),
        check_vma=False,
    )
```

```python
import functools
import math

import jax
import jax.numpy as jnp
from jax import lax
from jax.experimental import pallas as pl
from jax.experimental.pallas import tpu as pltpu
from jax.sharding import PartitionSpec as P

gelu_scale = 0.7978845608028654
gelu_cube = 0.044715
BF = jnp.bfloat16
F32 = jnp.float32
ANY = pl.BlockSpec(memory_space=pl.ANY)
VMEM_BYTES = 56 * 1024 * 1024
small_cost = pl.CostEstimate(flops=1000, bytes_accessed=1000, transcendentals=0)
stagger_cost = pl.CostEstimate(flops=3000000000, bytes_accessed=1000, transcendentals=0)


def gelu_pair(value):
    inner = gelu_scale * (value + gelu_cube * value * value * value)
    tangent = jnp.tanh(inner)
    result = 0.5 * value * (1.0 + tangent)
    slope = 0.5 * (1.0 + tangent) + 0.5 * value * (1.0 - tangent * tangent) * gelu_scale * (
        1.0 + 3.0 * gelu_cube * value * value
    )
    return (result, slope)


def line_pairs(line, step, first, last):
    return [
        (a * 2 + s, (a + step) * 2 + s)
        for a in range(first, last + 1)
        for s in range(2)
        if 0 <= a + step < line
    ]


def swap_pairs(first, last):
    return [(a * 2 + s, a * 2 + 1 - s) for a in range(first, last + 1) for s in range(2)]


def tie(value, others):
    return lax.optimization_barrier((value, others)) if others else (value, others)


def gather_parts(own, line):
    middle = line // 2
    held = {0: (own, own)}
    parts = [(own, 0, 0, 0, line - 1)]
    crossed, places, later = [], [], []
    for step in range(1, line + 1):
        k = step - 1
        (from_up, from_down), crossed = tie(held[k], crossed)
        for n, got in zip(places, crossed):
            parts[n] = (got,) + parts[n][1:]
        places = []
        if step < line:
            up = lax.ppermute(from_up, "tensor", line_pairs(line, 1, k, line - 2))
            down = lax.ppermute(from_down, "tensor", line_pairs(line, -1, 1, line - 1 - k))
            held[step] = (up, down)
            parts += [(up, -step, 0, step, line - 1), (down, step, 0, 0, line - 1 - step)]
        if k == 0:
            moves, after = [(own, 0, 0, line - 1)], []
        else:
            moves = [
                (from_down, k, 0, min(middle - 1, line - 1 - k)),
                (from_up, -k, max(middle, k), line - 1),
            ]
            after = [(from_up, -k, k, middle - 1), (from_down, k, middle, line - 1 - k)]
        crossed = []
        for value, d, first, last in moves + later:
            if first <= last:
                got = lax.ppermute(value, "tensor", swap_pairs(first, last))
                places.append(len(parts))
                parts.append((got, d, 1, first, last))
                crossed.append(got)
        later = after
    for value, d, first, last in later:
        if first <= last:
            got = lax.ppermute(value, "tensor", swap_pairs(first, last))
            parts.append((got, d, 1, first, last))
    return parts


class Order:
    def __init__(self, last):
        self.last = [last]

    def kernel(self, call, *args, also=()):
        out = call([*self.last, *also], *args)
        self.last = [jax.tree.leaves(out)[0]]
        return out


    def fusion(self, call, *args):
        args, before = tie(args, self.last)
        out = call(*args)
        self.last = [jax.tree.leaves(out)[0], *before]
        return out


def far_first(line):
    return sorted(range(line), key=lambda k: (-max(k, line - k) if k else 0, -k))


class LineSum:
    def __init__(self, keep, send):
        self.line, self.keep, self.k = keep.shape[0], keep, keep.shape[0] - 1
        self.got = [lax.ppermute(part, "tensor", swap_pairs(0, self.line - 1)) for part in send]
        self.moved = []

    def across(self, k):
        n = far_first(self.line).index(k)
        return self.got[2 * n // self.line], n % (self.line // 2)

    def step(self, order):
        k, line = self.k, self.line

        def both(k, keep, got):
            return keep[k].astype(F32) + got[self.across(k)[1]].astype(F32)

        if k > 0:

            def loads(keep, got_up, got_down, *moved):
                out = [both(k, keep, got_up), both(line - k, keep, got_down)]
                if moved:
                    out = [a + b.astype(F32) for a, b in zip(out, moved)]
                return [a.astype(BF) for a in out]

            got = self.across(k)[0], self.across(line - k)[0]
            up, down = order.fusion(loads, self.keep, *got, *self.moved)
            self.moved = [
                lax.ppermute(up, "tensor", line_pairs(line, 1, 0, line - 1 - k)),
                lax.ppermute(down, "tensor", line_pairs(line, -1, k, line - 1)),
            ]
        else:

            def last(keep, got, *moved):
                total = both(0, keep, got)
                for a in moved:
                    total = total + a.astype(F32)
                return total.astype(BF)

            self.total = order.fusion(last, self.keep, self.across(0)[0], *self.moved)
        self.k -= 1

    def finished(self):
        return self.k < 0


def core_swap(value):
    count = lax.axis_size("dp")
    return lax.ppermute(value, "dp", [(i, i ^ 1) for i in range(count)])


def ring_parts(value):
    count = lax.axis_size("dp")
    parts = [value]
    for t in range(2, count, 2):
        parts.append(lax.ppermute(value, "dp", [(i, (i + t) % count) for i in range(count)]))
    if len(parts) > 2:
        ring = lax.axis_index("dp") // 2
        stacked = jnp.stack(parts)
        parts = [
            lax.dynamic_index_in_dim(stacked, (ring - y) % len(parts), keepdims=False)
            for y in range(len(parts))
        ]
    return parts


def load_parts(meta, ranges, refs, full, sem):
    at, side = meta[0], meta[1]
    for (offset, other, first, last), ref in zip(ranges, refs):

        @pl.when((at >= first) & (at <= last))
        def _(offset=offset, other=other, ref=ref):
            slot = (at + offset) * 2 + (1 - side if other else side)
            pltpu.make_async_copy(ref, full.at[slot], sem).start()


def wait_parts(full, sem):
    pltpu.make_async_copy(full, full, sem).wait()


def block_at(pat, row, j, blocks, own_blocks, size):
    block = pat[row * blocks + j]
    return block // own_blocks, pl.ds(pl.multiple_of((block % own_blocks) * size, size), size)


def pick(full, pat, row, blocks, size):
    own_blocks = full.shape[-1] // size
    pieces = []
    for j in range(blocks):
        shard, lanes = block_at(pat, row, j, blocks, own_blocks, size)
        pieces.append(full[shard, :, lanes])
    return jnp.concatenate(pieces, axis=1)


def forward_kernel(ranges, meta, pat, *refs):
    parts, refs = refs[: len(ranges)], refs[len(ranges) :]
    w_ref, act_ref, slope_ref, full, sem = refs
    row = pl.program_id(0)

    @pl.when(row == 0)
    def _():
        load_parts(meta, ranges, parts, full, sem)
        wait_parts(full, sem)

    together, blocks, size, _ = w_ref.shape
    for i in range(together):
        picked = pick(full, pat, row * together + i, blocks, size)
        pre = jnp.dot(picked, w_ref[i].reshape(blocks * size, size), preferred_element_type=F32)
        value, slope = gelu_pair(pre)
        act_ref[i] = value.astype(BF)
        slope_ref[i] = slope


def forward(meta, pat, parts, weights, line):
    rows, blocks, size, _ = weights.shape
    parts, ranges = [p[0] for p in parts], [p[1:] for p in parts]
    tok, width = parts[0].shape
    shards = 2 * line
    together = math.gcd(rows, 8)
    spec = pl.BlockSpec((together, tok, size), lambda r, *_: (r, 0, 0))
    return pl.pallas_call(
        functools.partial(forward_kernel, ranges),
        grid_spec=pltpu.PrefetchScalarGridSpec(
            num_scalar_prefetch=2,
            grid=(rows // together,),
            in_specs=[ANY] * len(parts)
            + [pl.BlockSpec((together, blocks, size, size), lambda r, *_: (r, 0, 0, 0))],
            out_specs=[spec, spec],
            scratch_shapes=[pltpu.VMEM((shards, tok, width), BF), pltpu.SemaphoreType.DMA],
        ),
        out_shape=[
            jax.ShapeDtypeStruct((rows, tok, size), BF),
            jax.ShapeDtypeStruct((rows, tok, size), F32),
        ],
        compiler_params=pltpu.CompilerParams(vmem_limit_bytes=VMEM_BYTES),
        cost_estimate=stagger_cost,
        name="forward_rows",
    )(meta, pat, *parts, weights)


def spread_kernel(flip, n_after, line, meta, pat, *refs):
    in_ref, w_ref, *out_refs, acc = refs[n_after:]
    step = pl.program_id(0)
    together, blocks, size, _ = w_ref.shape
    own_blocks = acc.shape[-1] // size

    @pl.when(step == 0)
    def _():
        acc[...] = jnp.zeros_like(acc)

    for i in range(together):
        value = in_ref[i]
        if flip:
            weight = w_ref[i].reshape(blocks * size, size)
            terms = lax.dot_general(
                value, weight, (((1,), (1,)), ((), ())), preferred_element_type=F32
            )
        else:
            weight = jnp.concatenate([w_ref[i, j] for j in range(blocks)], axis=1)
            terms = jnp.dot(value, weight, preferred_element_type=F32)
        for j in range(blocks):
            shard, lanes = block_at(pat, step * together + i, j, blocks, own_blocks, size)
            acc[shard, :, lanes] += terms[:, j * size : (j + 1) * size]

    @pl.when(step == pl.num_programs(0) - 1)
    def _():
        keep_ref, *send_refs = out_refs
        at, side = meta[0], meta[1]
        for n, k in enumerate(far_first(line)):
            place = lax.rem(at + k, line) * 2
            keep_ref[k] = acc[place + side].astype(BF)
            send_refs[2 * n // line][n % (line // 2)] = acc[place + 1 - side].astype(BF)


def spread(flip, meta, pat, line, width, after, values, weights):
    rows, blocks, size, _ = weights.shape
    tok = values.shape[1]
    together = math.gcd(rows, 4)
    whole = (2 * line, tok, width)
    shapes = [(line, tok, width)] + [(line // 2, tok, width)] * 2
    return pl.pallas_call(
        functools.partial(spread_kernel, flip, len(after), line),
        grid_spec=pltpu.PrefetchScalarGridSpec(
            num_scalar_prefetch=2,
            grid=(rows // together,),
            in_specs=[
                *[ANY] * len(after),
                pl.BlockSpec((together, tok, size), lambda r, *_: (r, 0, 0)),
                pl.BlockSpec((together, blocks, size, size), lambda r, *_: (r, 0, 0, 0)),
            ],
            out_specs=[pl.BlockSpec(d, lambda r, *_, n=len(d): (0,) * n) for d in shapes],
            scratch_shapes=[pltpu.VMEM(whole, F32)],
        ),
        out_shape=[jax.ShapeDtypeStruct(d, BF) for d in shapes],
        compiler_params=pltpu.CompilerParams(vmem_limit_bytes=VMEM_BYTES),
        cost_estimate=small_cost,
        name="spread_back" if flip else "spread_out",
    )(meta, pat, *after, values, weights)


def chunk_row(start, half, meta, i, rows):
    core = meta[2] if half == 0 else 1 - meta[2]
    return core * (rows // 2) + start + i


def chunk_kernel(n_after, ranges, spans, start, half, rows, chained, meta, pat, *refs):
    refs = refs[n_after:]
    n = len(ranges)
    x_parts, g_parts, refs = refs[:n], refs[n : 2 * n], refs[2 * n :]
    act_ref, slope_ref, w_ref = refs[:3]
    more, refs = (refs[3 : 3 + 2 * len(spans)], refs[3 + 2 * len(spans) :]) if half == 0 else ((), refs[3:])
    refs = refs[1:] if chained else refs
    *outs, pg_ref, g_full, x_full, g_sem, x_sem = refs
    step = pl.program_id(0)
    together, blocks, size, _ = w_ref.shape
    row = chunk_row(start, half, meta, step * together, rows)

    @pl.when(step == 0)
    def _():
        load_parts(meta, ranges, g_parts, g_full, g_sem)
        load_parts(meta, ranges, x_parts, x_full, x_sem)
        wait_parts(g_full, g_sem)

    def store(n, which, i, terms):
        for j, term in enumerate(terms):
            if half == 0:
                term = term.astype(F32) + more[2 * n + which][i, j].astype(F32)
                outs[n][which, i, j] = term.astype(BF)
            else:
                outs[2 * n + which][i, j] = term

    def work(n):
        for i in range(together):
            grads = pick(g_full, pat, row + i, blocks, size)
            second = lax.dot_general(
                act_ref[i], grads, (((0,), (0,)), ((), ())), preferred_element_type=F32
            ).astype(BF)
            store(n, 0, i, [second[:, j * size : (j + 1) * size] for j in range(blocks)])
            weight = jnp.concatenate([w_ref[i, j] for j in range(blocks)], axis=1)
            act_grad = lax.dot_general(
                grads, weight, (((1,), (1,)), ((), ())), preferred_element_type=F32
            )
            pg_ref[i] = (act_grad * slope_ref[i]).astype(BF)
        if n == 0:

            @pl.when(step == 0)
            def _():
                wait_parts(x_full, x_sem)

        for i in range(together):
            picked = pick(x_full, pat, row + i, blocks, size)
            first = lax.dot_general(
                picked, pg_ref[i], (((0,), (0,)), ((), ())), preferred_element_type=F32
            ).astype(BF)
            store(n, 1, i, [first[j * size : (j + 1) * size] for j in range(blocks)])

    if len(spans) == 1:
        return work(0)
    for n, (low, count) in enumerate(spans):
        inside = (step >= low // together) & (step < (low + count) // together)
        pl.when(inside)(functools.partial(work, n))


def chunk(meta, pat, x_parts, g_parts, act, slope, weights, line, start, counts, half, after, more, pg):
    rows, blocks, size, _ = weights.shape
    ranges = [p[1:] for p in x_parts]
    parts = [p[0] for p in x_parts + g_parts]
    tok, width = parts[0].shape
    spans = [(sum(counts[:n]), count) for n, count in enumerate(counts)]
    together = math.gcd(start, rows // 2, 4, *counts)

    def at_row(r, meta, pat):
        return (chunk_row(start, half, meta, r * together, rows) // together, 0, 0)

    def in_span(low, count, lead):
        def index(r, *_):
            return lead + (jnp.clip(r - low // together, 0, count // together - 1), 0, 0, 0)

        return pl.BlockSpec((2,) * len(lead) + (together, blocks, size, size), index)

    row_spec = pl.BlockSpec((together, tok, size), at_row)
    w_spec = pl.BlockSpec((together, blocks, size, size), lambda r, m, p: at_row(r, m, p) + (0,))
    args = [*after, *parts, act, slope, weights]
    specs = [ANY] * (len(after) + len(parts)) + [row_spec, row_spec, w_spec]
    out_specs, out_shape = [], []
    for low, count in spans:
        if half == 0:
            specs += [in_span(low, count, ())] * 2
            out_specs.append(in_span(low, count, (0,)))
            out_shape.append(jax.ShapeDtypeStruct((2, count, blocks, size, size), BF))
        else:
            out_specs += [in_span(low, count, ())] * 2
            out_shape += [jax.ShapeDtypeStruct((count, blocks, size, size), BF)] * 2
    if half == 0:
        args += more
    aliases = {}
    if pg is not None:
        aliases = {2 + len(args): len(out_shape)}
        args.append(pg)
        specs.append(ANY)
    full = pltpu.VMEM((2 * line, tok, width), BF)
    *outs, pg = pl.pallas_call(
        functools.partial(
            chunk_kernel, len(after), ranges, spans, start, half, rows, pg is not None
        ),
        grid_spec=pltpu.PrefetchScalarGridSpec(
            num_scalar_prefetch=2,
            grid=(sum(counts) // together,),
            in_specs=specs,
            out_specs=out_specs + [row_spec],
            scratch_shapes=[full, full, pltpu.SemaphoreType.DMA, pltpu.SemaphoreType.DMA],
        ),
        out_shape=out_shape + [jax.ShapeDtypeStruct((rows, tok, size), BF)],
        input_output_aliases=aliases,
        compiler_params=pltpu.CompilerParams(vmem_limit_bytes=VMEM_BYTES),
        cost_estimate=small_cost,
        name="grad_rows",
    )(meta, pat, *args)
    return outs, pg


def place_kernel(n_after, total, chained, meta, *refs):
    refs = refs[n_after:]
    in_refs, refs = refs[:total], refs[total + (2 if chained else 0) + 1 :]
    for which in range(2):
        if len(refs) == 2:
            value = in_refs[which][...]
        else:
            value = in_refs[0][which].astype(F32)
            for ref in in_refs[1:]:
                value = value + ref[which].astype(F32)
            value = value.astype(BF)
            refs[2 + which][...] = value
        refs[which][...] = value


def place(meta, shape, start, half, after, parts, into):
    rows, blocks, size, _ = shape
    adding = half == 0
    count = parts[0].shape[1 if adding else 0]
    together = math.gcd(count, start, 2, rows // 2)
    n = len(parts)

    def at_row(r, meta):
        return (chunk_row(start, half, meta, r * together, rows) // together, 0, 0, 0)

    pair_spec = pl.BlockSpec((2, together, blocks, size, size), lambda r, *_: (0, r, 0, 0, 0))
    one_spec = pl.BlockSpec((together, blocks, size, size), lambda r, *_: (r, 0, 0, 0))
    out_spec = pl.BlockSpec((together, blocks, size, size), at_row)
    out_shape = [jax.ShapeDtypeStruct((8, 128), jnp.int32)] + [jax.ShapeDtypeStruct(shape, BF)] * 2
    out_specs = [ANY, out_spec, out_spec]
    if adding:
        out_shape += [jax.ShapeDtypeStruct(parts[0].shape[1:], BF)] * 2
        out_specs += [one_spec, one_spec]
    args = [*after, *parts]
    specs = [ANY] * len(after) + [pair_spec if adding else one_spec] * n
    aliases = {}
    if into is not None:
        aliases = {1 + len(args): 1, 2 + len(args): 2}
        args += into
        specs += [ANY, ANY]
    _, second, first, *own = pl.pallas_call(
        functools.partial(place_kernel, len(after), n, into is not None),
        grid_spec=pltpu.PrefetchScalarGridSpec(
            num_scalar_prefetch=1,
            grid=(count // together,),
            in_specs=specs,
            out_specs=out_specs,
        ),
        out_shape=out_shape,
        input_output_aliases=aliases,
        compiler_params=pltpu.CompilerParams(vmem_limit_bytes=VMEM_BYTES),
        cost_estimate=small_cost,
        name="place_rows",
    )(meta, *args)
    return _, [second, first], own


def chunk_counts(half_rows):
    unit = half_rows // 8
    if unit and half_rows == 8 * unit:
        return [2 * unit, 3 * unit, 2 * unit, unit]
    return [1] * half_rows


def shards(tokens, pattern, first_blocks, second_blocks, out_grad):
    rows, blocks, size, _ = first_blocks.shape
    width = tokens.shape[1]
    line = lax.axis_size("tensor") // 2
    where = lax.axis_index("tensor")
    core = lax.axis_index("dp") % 2
    meta = jnp.stack([where // 2, where % 2, core]).astype(jnp.int32)
    pat = pattern.reshape(-1)

    half_rows = rows // 2
    counts = chunk_counts(half_rows)
    starts = [sum(counts[:n]) for n in range(len(counts))]
    chunks = range(len(counts))

    x_parts, g_parts = gather_parts(tokens, line), gather_parts(out_grad, line)
    act, slope = forward(meta, pat, x_parts, first_blocks, line)
    order = Order(act)

    def grad_rows(first, last, half, more, pg):
        run = functools.partial(
            chunk, meta, pat, x_parts, g_parts, act, slope, second_blocks, line, starts[first],
            counts[first:last], half,
        )
        return order.kernel(run, more, pg)

    def sum_half(first, last, pg):
        outs, pg = grad_rows(first, last, 0, [s for pair in sent[first:last] for s in pair], pg)
        if first > 0:
            outs[0], kept[0][1:] = tie(outs[0], kept[0][1:])
        return [ring_parts(grads) for grads in outs], pg

    def other_half(first, last, pg):
        outs, pg = grad_rows(first, last, 1, None, pg)
        swapped = [core_swap(grads) for grads in outs]
        return [swapped[n : n + 2] for n in range(0, len(swapped), 2)], pg

    last = len(counts)
    sums = []

    def spread_rows(flip, values, weights):
        run = functools.partial(spread, flip, meta, pat, line, width)
        keep, *send = order.kernel(run, values, weights)
        sums.append(LineSum(keep, send))

    sent, pg = other_half(0, 1, None)
    kept, pg = sum_half(0, 1, pg)
    if last > 1:
        more, pg = other_half(1, last, pg)
        sent += more
    spread_rows(False, act, second_blocks)
    if last > 1:
        more, pg = sum_half(1, last, pg)
        kept += more

    totals, own = None, {}

    def settle(n, totals, also=()):
        run = functools.partial(place, meta, first_blocks.shape, starts[n], 0)
        _, totals, one = order.kernel(run, kept[n], totals, also=also)
        own[n] = [core_swap(v) for v in one]
        return totals

    def settle_other(n, totals):
        run = functools.partial(place, meta, first_blocks.shape, starts[n], 1)
        return order.kernel(run, own[n], totals)[1]

    totals = settle(0, totals)
    spread_rows(True, pg, first_blocks)
    out, back = sums
    while out.k > 0:
        out.step(order)
    back.step(order)
    for n in range(1, last):
        totals = settle(n, totals)
        if n < last - 1:
            for item in (out, back):
                if not item.finished():
                    item.step(order)
            totals = settle_other(n - 1, totals)
    for n in range(max(last - 2, 0), last):
        totals = settle_other(n, totals)
    for item in (out, back):
        while not item.finished():
            item.step(order)
    return (out.total, back.total, totals[1], totals[0])


def solution(mesh):
    placed = (
        P("dp", "tensor"),
        P("tensor", None),
        P("tensor", None, None, None),
        P("tensor", None, None, None),
        P("dp", "tensor"),
    )
    return jax.shard_map(
        shards,
        mesh=mesh,
        in_specs=placed,
        out_specs=(
            P("dp", "tensor"),
            P("dp", "tensor"),
            P("tensor", None, None, None),
            P("tensor", None, None, None),
        ),
        check_vma=False,
    )
```

```python
import functools
import math

import jax
import jax.numpy as jnp
from jax import lax
from jax.experimental import pallas as pl
from jax.experimental.pallas import tpu as pltpu
from jax.sharding import PartitionSpec as P

gelu_scale = 0.7978845608028654
gelu_cube = 0.044715
BF = jnp.bfloat16
F32 = jnp.float32
ANY = pl.BlockSpec(memory_space=pl.ANY)
VMEM_BYTES = 56 * 1024 * 1024
small_cost = pl.CostEstimate(flops=1000, bytes_accessed=1000, transcendentals=0)
stagger_cost = pl.CostEstimate(flops=3000000000, bytes_accessed=1000, transcendentals=0)


def gelu_pair(value):
    inner = gelu_scale * (value + gelu_cube * value * value * value)
    tangent = jnp.tanh(inner)
    result = 0.5 * value * (1.0 + tangent)
    slope = 0.5 * (1.0 + tangent) + 0.5 * value * (1.0 - tangent * tangent) * gelu_scale * (
        1.0 + 3.0 * gelu_cube * value * value
    )
    return (result, slope)


def line_pairs(line, step, first, last):
    return [
        (a * 2 + s, (a + step) * 2 + s)
        for a in range(first, last + 1)
        for s in range(2)
        if 0 <= a + step < line
    ]


def swap_pairs(first, last):
    return [(a * 2 + s, a * 2 + 1 - s) for a in range(first, last + 1) for s in range(2)]


def tie(value, others):
    return lax.optimization_barrier((value, others)) if others else (value, others)


def gather_parts(own, line):
    middle = line // 2
    held = {0: (own, own)}
    parts = [(own, 0, 0, 0, line - 1)]
    crossed, places, later = [], [], []
    for step in range(1, line + 1):
        k = step - 1
        (from_up, from_down), crossed = tie(held[k], crossed)
        for n, got in zip(places, crossed):
            parts[n] = (got,) + parts[n][1:]
        places = []
        if step < line:
            up = lax.ppermute(from_up, "tensor", line_pairs(line, 1, k, line - 2))
            down = lax.ppermute(from_down, "tensor", line_pairs(line, -1, 1, line - 1 - k))
            held[step] = (up, down)
            parts += [(up, -step, 0, step, line - 1), (down, step, 0, 0, line - 1 - step)]
        if k == 0:
            moves, after = [(own, 0, 0, line - 1)], []
        else:
            moves = [
                (from_down, k, 0, min(middle - 1, line - 1 - k)),
                (from_up, -k, max(middle, k), line - 1),
            ]
            after = [(from_up, -k, k, middle - 1), (from_down, k, middle, line - 1 - k)]
        crossed = []
        for value, d, first, last in moves + later:
            if first <= last:
                got = lax.ppermute(value, "tensor", swap_pairs(first, last))
                places.append(len(parts))
                parts.append((got, d, 1, first, last))
                crossed.append(got)
        later = after
    for value, d, first, last in later:
        if first <= last:
            got = lax.ppermute(value, "tensor", swap_pairs(first, last))
            parts.append((got, d, 1, first, last))
    return parts


class Order:
    def __init__(self, last):
        self.last = [last]

    def kernel(self, call, *args, also=()):
        out = call([*self.last, *also], *args)
        self.last = [jax.tree.leaves(out)[0]]
        return out


    def fusion(self, call, *args):
        args, before = tie(args, self.last)
        out = call(*args)
        self.last = [jax.tree.leaves(out)[0], *before]
        return out


def far_first(line):
    return sorted(range(line), key=lambda k: (-max(k, line - k) if k else 0, -k))


class LineSum:
    def __init__(self, keep, send):
        self.line, self.keep, self.k = keep.shape[0], keep, keep.shape[0] - 1
        self.got = [lax.ppermute(part, "tensor", swap_pairs(0, self.line - 1)) for part in send]
        self.moved = []

    def across(self, k):
        n = far_first(self.line).index(k)
        return self.got[2 * n // self.line], n % (self.line // 2)

    def step(self, order):
        k, line = self.k, self.line

        def both(k, keep, got):
            return keep[k].astype(F32) + got[self.across(k)[1]].astype(F32)

        if k > 0:

            def loads(keep, got_up, got_down, *moved):
                out = [both(k, keep, got_up), both(line - k, keep, got_down)]
                if moved:
                    out = [a + b.astype(F32) for a, b in zip(out, moved)]
                return [a.astype(BF) for a in out]

            got = self.across(k)[0], self.across(line - k)[0]
            up, down = order.fusion(loads, self.keep, *got, *self.moved)
            self.moved = [
                lax.ppermute(up, "tensor", line_pairs(line, 1, 0, line - 1 - k)),
                lax.ppermute(down, "tensor", line_pairs(line, -1, k, line - 1)),
            ]
        else:

            def last(keep, got, *moved):
                total = both(0, keep, got)
                for a in moved:
                    total = total + a.astype(F32)
                return total.astype(BF)

            self.total = order.fusion(last, self.keep, self.across(0)[0], *self.moved)
        self.k -= 1

    def finished(self):
        return self.k < 0


def core_swap(value):
    count = lax.axis_size("dp")
    return lax.ppermute(value, "dp", [(i, i ^ 1) for i in range(count)])


def ring_parts(value):
    count = lax.axis_size("dp")
    parts = [value]
    for t in range(2, count, 2):
        parts.append(lax.ppermute(value, "dp", [(i, (i + t) % count) for i in range(count)]))
    if len(parts) > 2:
        ring = lax.axis_index("dp") // 2
        stacked = jnp.stack(parts)
        parts = [
            lax.dynamic_index_in_dim(stacked, (ring - y) % len(parts), keepdims=False)
            for y in range(len(parts))
        ]
    return parts


def load_parts(meta, ranges, refs, full, sem):
    at, side = meta[0], meta[1]
    for (offset, other, first, last), ref in zip(ranges, refs):

        @pl.when((at >= first) & (at <= last))
        def _(offset=offset, other=other, ref=ref):
            slot = (at + offset) * 2 + (1 - side if other else side)
            pltpu.make_async_copy(ref, full.at[slot], sem).start()


def wait_parts(full, sem):
    pltpu.make_async_copy(full, full, sem).wait()


def block_at(pat, row, j, blocks, own_blocks, size):
    block = pat[row * blocks + j]
    return block // own_blocks, pl.ds(pl.multiple_of((block % own_blocks) * size, size), size)


def pick(full, pat, row, blocks, size):
    own_blocks = full.shape[-1] // size
    pieces = []
    for j in range(blocks):
        shard, lanes = block_at(pat, row, j, blocks, own_blocks, size)
        pieces.append(full[shard, :, lanes])
    return jnp.concatenate(pieces, axis=1)


def forward_kernel(ranges, meta, pat, *refs):
    parts, refs = refs[: len(ranges)], refs[len(ranges) :]
    w_ref, act_ref, slope_ref, full, sem = refs
    row = pl.program_id(0)

    @pl.when(row == 0)
    def _():
        load_parts(meta, ranges, parts, full, sem)
        wait_parts(full, sem)

    together, blocks, size, _ = w_ref.shape
    for i in range(together):
        picked = pick(full, pat, row * together + i, blocks, size)
        pre = jnp.dot(picked, w_ref[i].reshape(blocks * size, size), preferred_element_type=F32)
        value, slope = gelu_pair(pre)
        act_ref[i] = value.astype(BF)
        slope_ref[i] = slope


def forward(meta, pat, parts, weights, line):
    rows, blocks, size, _ = weights.shape
    parts, ranges = [p[0] for p in parts], [p[1:] for p in parts]
    tok, width = parts[0].shape
    shards = 2 * line
    together = math.gcd(rows, 8)
    spec = pl.BlockSpec((together, tok, size), lambda r, *_: (r, 0, 0))
    return pl.pallas_call(
        functools.partial(forward_kernel, ranges),
        grid_spec=pltpu.PrefetchScalarGridSpec(
            num_scalar_prefetch=2,
            grid=(rows // together,),
            in_specs=[ANY] * len(parts)
            + [pl.BlockSpec((together, blocks, size, size), lambda r, *_: (r, 0, 0, 0))],
            out_specs=[spec, spec],
            scratch_shapes=[pltpu.VMEM((shards, tok, width), BF), pltpu.SemaphoreType.DMA],
        ),
        out_shape=[
            jax.ShapeDtypeStruct((rows, tok, size), BF),
            jax.ShapeDtypeStruct((rows, tok, size), F32),
        ],
        compiler_params=pltpu.CompilerParams(vmem_limit_bytes=VMEM_BYTES),
        cost_estimate=stagger_cost,
        name="forward_rows",
    )(meta, pat, *parts, weights)


def spread_kernel(flip, n_after, line, meta, pat, *refs):
    in_ref, w_ref, *out_refs, acc = refs[n_after:]
    step = pl.program_id(0)
    together, blocks, size, _ = w_ref.shape
    own_blocks = acc.shape[-1] // size

    @pl.when(step == 0)
    def _():
        acc[...] = jnp.zeros_like(acc)

    for i in range(together):
        value = in_ref[i]
        if flip:
            weight = w_ref[i].reshape(blocks * size, size)
            terms = lax.dot_general(
                value, weight, (((1,), (1,)), ((), ())), preferred_element_type=F32
            )
        else:
            weight = jnp.concatenate([w_ref[i, j] for j in range(blocks)], axis=1)
            terms = jnp.dot(value, weight, preferred_element_type=F32)
        for j in range(blocks):
            shard, lanes = block_at(pat, step * together + i, j, blocks, own_blocks, size)
            acc[shard, :, lanes] += terms[:, j * size : (j + 1) * size]

    @pl.when(step == pl.num_programs(0) - 1)
    def _():
        keep_ref, *send_refs = out_refs
        at, side = meta[0], meta[1]
        for n, k in enumerate(far_first(line)):
            place = lax.rem(at + k, line) * 2
            keep_ref[k] = acc[place + side].astype(BF)
            send_refs[2 * n // line][n % (line // 2)] = acc[place + 1 - side].astype(BF)


def spread(flip, meta, pat, line, width, after, values, weights):
    rows, blocks, size, _ = weights.shape
    tok = values.shape[1]
    together = math.gcd(rows, 4)
    whole = (2 * line, tok, width)
    shapes = [(line, tok, width)] + [(line // 2, tok, width)] * 2
    return pl.pallas_call(
        functools.partial(spread_kernel, flip, len(after), line),
        grid_spec=pltpu.PrefetchScalarGridSpec(
            num_scalar_prefetch=2,
            grid=(rows // together,),
            in_specs=[
                *[ANY] * len(after),
                pl.BlockSpec((together, tok, size), lambda r, *_: (r, 0, 0)),
                pl.BlockSpec((together, blocks, size, size), lambda r, *_: (r, 0, 0, 0)),
            ],
            out_specs=[pl.BlockSpec(d, lambda r, *_, n=len(d): (0,) * n) for d in shapes],
            scratch_shapes=[pltpu.VMEM(whole, F32)],
        ),
        out_shape=[jax.ShapeDtypeStruct(d, BF) for d in shapes],
        compiler_params=pltpu.CompilerParams(vmem_limit_bytes=VMEM_BYTES),
        cost_estimate=small_cost,
        name="spread_back" if flip else "spread_out",
    )(meta, pat, *after, values, weights)


def chunk_row(start, half, meta, i, rows):
    core = meta[2] if half == 0 else 1 - meta[2]
    return core * (rows // 2) + start + i


def chunk_kernel(n_after, ranges, spans, start, half, rows, chained, meta, pat, *refs):
    refs = refs[n_after:]
    n = len(ranges)
    x_parts, g_parts, refs = refs[:n], refs[n : 2 * n], refs[2 * n :]
    act_ref, slope_ref, w_ref = refs[:3]
    more, refs = (refs[3 : 3 + 2 * len(spans)], refs[3 + 2 * len(spans) :]) if half == 0 else ((), refs[3:])
    refs = refs[1:] if chained else refs
    *outs, pg_ref, g_full, x_full, g_sem, x_sem = refs
    step = pl.program_id(0)
    together, blocks, size, _ = w_ref.shape
    row = chunk_row(start, half, meta, step * together, rows)

    @pl.when(step == 0)
    def _():
        load_parts(meta, ranges, g_parts, g_full, g_sem)
        load_parts(meta, ranges, x_parts, x_full, x_sem)
        wait_parts(g_full, g_sem)

    def store(n, which, i, terms):
        for j, term in enumerate(terms):
            if half == 0:
                term = term.astype(F32) + more[2 * n + which][i, j].astype(F32)
                outs[n][which, i, j] = term.astype(BF)
            else:
                outs[2 * n + which][i, j] = term

    def work(n):
        for i in range(together):
            grads = pick(g_full, pat, row + i, blocks, size)
            second = lax.dot_general(
                act_ref[i], grads, (((0,), (0,)), ((), ())), preferred_element_type=F32
            ).astype(BF)
            store(n, 0, i, [second[:, j * size : (j + 1) * size] for j in range(blocks)])
            weight = jnp.concatenate([w_ref[i, j] for j in range(blocks)], axis=1)
            act_grad = lax.dot_general(
                grads, weight, (((1,), (1,)), ((), ())), preferred_element_type=F32
            )
            pg_ref[i] = (act_grad * slope_ref[i]).astype(BF)
        if n == 0:

            @pl.when(step == 0)
            def _():
                wait_parts(x_full, x_sem)

        for i in range(together):
            picked = pick(x_full, pat, row + i, blocks, size)
            first = lax.dot_general(
                picked, pg_ref[i], (((0,), (0,)), ((), ())), preferred_element_type=F32
            ).astype(BF)
            store(n, 1, i, [first[j * size : (j + 1) * size] for j in range(blocks)])

    if len(spans) == 1:
        return work(0)
    for n, (low, count) in enumerate(spans):
        inside = (step >= low // together) & (step < (low + count) // together)
        pl.when(inside)(functools.partial(work, n))


def chunk(meta, pat, x_parts, g_parts, act, slope, weights, line, start, counts, half, after, more, pg):
    rows, blocks, size, _ = weights.shape
    ranges = [p[1:] for p in x_parts]
    parts = [p[0] for p in x_parts + g_parts]
    tok, width = parts[0].shape
    spans = [(sum(counts[:n]), count) for n, count in enumerate(counts)]
    together = math.gcd(start, rows // 2, 4, *counts)

    def at_row(r, meta, pat):
        return (chunk_row(start, half, meta, r * together, rows) // together, 0, 0)

    def in_span(low, count, lead):
        def index(r, *_):
            return lead + (jnp.clip(r - low // together, 0, count // together - 1), 0, 0, 0)

        return pl.BlockSpec((2,) * len(lead) + (together, blocks, size, size), index)

    row_spec = pl.BlockSpec((together, tok, size), at_row)
    w_spec = pl.BlockSpec((together, blocks, size, size), lambda r, m, p: at_row(r, m, p) + (0,))
    args = [*after, *parts, act, slope, weights]
    specs = [ANY] * (len(after) + len(parts)) + [row_spec, row_spec, w_spec]
    out_specs, out_shape = [], []
    for low, count in spans:
        if half == 0:
            specs += [in_span(low, count, ())] * 2
            out_specs.append(in_span(low, count, (0,)))
            out_shape.append(jax.ShapeDtypeStruct((2, count, blocks, size, size), BF))
        else:
            out_specs += [in_span(low, count, ())] * 2
            out_shape += [jax.ShapeDtypeStruct((count, blocks, size, size), BF)] * 2
    if half == 0:
        args += more
    aliases = {}
    if pg is not None:
        aliases = {2 + len(args): len(out_shape)}
        args.append(pg)
        specs.append(ANY)
    full = pltpu.VMEM((2 * line, tok, width), BF)
    *outs, pg = pl.pallas_call(
        functools.partial(
            chunk_kernel, len(after), ranges, spans, start, half, rows, pg is not None
        ),
        grid_spec=pltpu.PrefetchScalarGridSpec(
            num_scalar_prefetch=2,
            grid=(sum(counts) // together,),
            in_specs=specs,
            out_specs=out_specs + [row_spec],
            scratch_shapes=[full, full, pltpu.SemaphoreType.DMA, pltpu.SemaphoreType.DMA],
        ),
        out_shape=out_shape + [jax.ShapeDtypeStruct((rows, tok, size), BF)],
        input_output_aliases=aliases,
        compiler_params=pltpu.CompilerParams(vmem_limit_bytes=VMEM_BYTES),
        cost_estimate=small_cost,
        name="grad_rows",
    )(meta, pat, *args)
    return outs, pg


def place_kernel(n_after, total, chained, meta, *refs):
    refs = refs[n_after:]
    in_refs, refs = refs[:total], refs[total + (2 if chained else 0) + 1 :]
    for which in range(2):
        if len(refs) == 2:
            value = in_refs[which][...]
        else:
            value = in_refs[0][which].astype(F32)
            for ref in in_refs[1:]:
                value = value + ref[which].astype(F32)
            value = value.astype(BF)
            refs[2 + which][...] = value
        refs[which][...] = value


def place(meta, shape, start, half, after, parts, into):
    rows, blocks, size, _ = shape
    adding = half == 0
    count = parts[0].shape[1 if adding else 0]
    together = math.gcd(count, start, 2, rows // 2)
    n = len(parts)

    def at_row(r, meta):
        return (chunk_row(start, half, meta, r * together, rows) // together, 0, 0, 0)

    pair_spec = pl.BlockSpec((2, together, blocks, size, size), lambda r, *_: (0, r, 0, 0, 0))
    one_spec = pl.BlockSpec((together, blocks, size, size), lambda r, *_: (r, 0, 0, 0))
    out_spec = pl.BlockSpec((together, blocks, size, size), at_row)
    out_shape = [jax.ShapeDtypeStruct((8, 128), jnp.int32)] + [jax.ShapeDtypeStruct(shape, BF)] * 2
    out_specs = [ANY, out_spec, out_spec]
    if adding:
        out_shape += [jax.ShapeDtypeStruct(parts[0].shape[1:], BF)] * 2
        out_specs += [one_spec, one_spec]
    args = [*after, *parts]
    specs = [ANY] * len(after) + [pair_spec if adding else one_spec] * n
    aliases = {}
    if into is not None:
        aliases = {1 + len(args): 1, 2 + len(args): 2}
        args += into
        specs += [ANY, ANY]
    _, second, first, *own = pl.pallas_call(
        functools.partial(place_kernel, len(after), n, into is not None),
        grid_spec=pltpu.PrefetchScalarGridSpec(
            num_scalar_prefetch=1,
            grid=(count // together,),
            in_specs=specs,
            out_specs=out_specs,
        ),
        out_shape=out_shape,
        input_output_aliases=aliases,
        compiler_params=pltpu.CompilerParams(vmem_limit_bytes=VMEM_BYTES),
        cost_estimate=small_cost,
        name="place_rows",
    )(meta, *args)
    return _, [second, first], own


def chunk_counts(half_rows):
    unit = half_rows // 8
    if unit and half_rows == 8 * unit:
        return [2 * unit, 3 * unit, 3 * unit]
    return [1] * half_rows


def shards(tokens, pattern, first_blocks, second_blocks, out_grad):
    rows, blocks, size, _ = first_blocks.shape
    width = tokens.shape[1]
    line = lax.axis_size("tensor") // 2
    where = lax.axis_index("tensor")
    core = lax.axis_index("dp") % 2
    meta = jnp.stack([where // 2, where % 2, core]).astype(jnp.int32)
    pat = pattern.reshape(-1)

    half_rows = rows // 2
    counts = chunk_counts(half_rows)
    starts = [sum(counts[:n]) for n in range(len(counts))]
    chunks = range(len(counts))

    x_parts, g_parts = gather_parts(tokens, line), gather_parts(out_grad, line)
    act, slope = forward(meta, pat, x_parts, first_blocks, line)
    order = Order(act)

    def grad_rows(first, last, half, more, pg):
        run = functools.partial(
            chunk, meta, pat, x_parts, g_parts, act, slope, second_blocks, line, starts[first],
            counts[first:last], half,
        )
        return order.kernel(run, more, pg)

    def sum_half(first, last, pg):
        outs, pg = grad_rows(first, last, 0, [s for pair in sent[first:last] for s in pair], pg)
        if first > 0:
            outs[0], kept[0][1:] = tie(outs[0], kept[0][1:])
        return [ring_parts(grads) for grads in outs], pg

    def other_half(first, last, pg):
        outs, pg = grad_rows(first, last, 1, None, pg)
        swapped = [core_swap(grads) for grads in outs]
        return [swapped[n : n + 2] for n in range(0, len(swapped), 2)], pg

    last = len(counts)
    sums = []

    def spread_rows(flip, values, weights):
        run = functools.partial(spread, flip, meta, pat, line, width)
        keep, *send = order.kernel(run, values, weights)
        sums.append(LineSum(keep, send))

    sent, pg = other_half(0, 1, None)
    kept, pg = sum_half(0, 1, pg)
    if last > 1:
        more, pg = other_half(1, last, pg)
        sent += more
    spread_rows(False, act, second_blocks)
    if last > 1:
        more, pg = sum_half(1, last, pg)
        kept += more

    totals, own = None, {}

    def settle(n, totals, also=()):
        run = functools.partial(place, meta, first_blocks.shape, starts[n], 0)
        _, totals, one = order.kernel(run, kept[n], totals, also=also)
        own[n] = [core_swap(v) for v in one]
        return totals

    def settle_other(n, totals):
        run = functools.partial(place, meta, first_blocks.shape, starts[n], 1)
        return order.kernel(run, own[n], totals)[1]

    totals = settle(0, totals)
    spread_rows(True, pg, first_blocks)
    out, back = sums
    while out.k > 0:
        out.step(order)
    back.step(order)
    for n in range(1, last):
        totals = settle(n, totals)
        if n == 1:
            out.step(order)
            back.step(order)
            totals = settle_other(0, totals)
            while not back.finished():
                back.step(order)
        if n > 1 or last == 2:
            totals = settle_other(n - 1, totals)
    totals = settle_other(last - 1, totals)
    for item in (out, back):
        while not item.finished():
            item.step(order)
    return (out.total, back.total, totals[1], totals[0])


def solution(mesh):
    placed = (
        P("dp", "tensor"),
        P("tensor", None),
        P("tensor", None, None, None),
        P("tensor", None, None, None),
        P("dp", "tensor"),
    )
    return jax.shard_map(
        shards,
        mesh=mesh,
        in_specs=placed,
        out_specs=(
            P("dp", "tensor"),
            P("dp", "tensor"),
            P("tensor", None, None, None),
            P("tensor", None, None, None),
        ),
        check_vma=False,
    )
```
